32 devices in a mesh: dp: 16 (over z, y, x), grp: 2 (over core).
Axes of the slice: x: 2, y: 2, z: 4, core: 2. Of those that a mesh axis runs over, the one named last changes fastest.
Arguments:
- tokens: bfloat16 [32, 512, 1152], P('dp', 'grp'), may hold values from -6 to 6
- cotangent: bfloat16 [32, 512, 1152], P('dp', 'grp'), may hold values from -6 to 6
- condition: float32 [24, 1152], P(None, 'dp'), may hold values from -6 to 6
- latent_of: int32 [32], P('dp'), may hold values from 0 to 23, as said below
- slot_valid: int32 [32], P('dp'), may hold values from 0 to 1, as said below
- ada_weight: float32 [1152, 6912], P('dp', 'grp'), may hold values from -0.1875 to 0.1875
- ada_weight_mean: float32 [1152, 6912], P('dp', 'grp'), may hold values from -0.03125 to 0.03125
- ada_weight_square: float32 [1152, 6912], P('dp', 'grp'), may hold values from 2e-06 to 1e-05
- ada_offset: float32 [6912], P('grp'), may hold values from -0.75 to 0.75
- ada_offset_mean: float32 [6912], P('grp'), may hold values from -0.03125 to 0.03125
- ada_offset_square: float32 [6912], P('grp'), may hold values from 2e-06 to 1e-05
- qkv_weight: float32 [1152, 3456], P('dp', 'grp'), may hold values from -0.1875 to 0.1875
- qkv_weight_mean: float32 [1152, 3456], P('dp', 'grp'), may hold values from -0.03125 to 0.03125
- qkv_weight_square: float32 [1152, 3456], P('dp', 'grp'), may hold values from 2e-06 to 1e-05
- proj_weight: float32 [1152, 1152], P('dp', 'grp'), may hold values from -0.5 to 0.5
- proj_weight_mean: float32 [1152, 1152], P('dp', 'grp'), may hold values from -0.03125 to 0.03125
- proj_weight_square: float32 [1152, 1152], P('dp', 'grp'), may hold values from 2e-06 to 1e-05
- up_weight: float32 [1152, 4608], P('dp', 'grp'), may hold values from -1 to 1
- up_weight_mean: float32 [1152, 4608], P('dp', 'grp'), may hold values from -0.03125 to 0.03125
- up_weight_square: float32 [1152, 4608], P('dp', 'grp'), may hold values from 2e-06 to 1e-05
- down_weight: float32 [4608, 1152], P('dp', 'grp'), may hold values from -0.375 to 0.375
- down_weight_mean: float32 [4608, 1152], P('dp', 'grp'), may hold values from -0.03125 to 0.03125
- down_weight_square: float32 [4608, 1152], P('dp', 'grp'), may hold values from 2e-06 to 1e-05
- main_bias: float32 [9216], P(('dp', 'grp')), may hold values from -0.75 to 0.75
- main_bias_mean: float32 [9216], P(('dp', 'grp')), may hold values from -0.03125 to 0.03125
- main_bias_square: float32 [9216], P(('dp', 'grp')), may hold values from 2e-06 to 1e-05
Outputs:
- block_out: bfloat16 [32, 512, 1152], P('dp', 'grp')
- tokens_grad: bfloat16 [32, 512, 1152], P('dp', 'grp')
- condition_grad: float32 [24, 1152], P(None, 'dp')
- ada_weight_grad: float32 [1152, 6912], P('dp', 'grp')
- ada_weight_new: float32 [1152, 6912], P('dp', 'grp')
- ada_weight_mean_new: float32 [1152, 6912], P('dp', 'grp')
- ada_weight_square_new: float32 [1152, 6912], P('dp', 'grp')
- ada_offset_grad: float32 [6912], P('grp')
- ada_offset_new: float32 [6912], P('grp')
- ada_offset_mean_new: float32 [6912], P('grp')
- ada_offset_square_new: float32 [6912], P('grp')
- qkv_weight_grad: float32 [1152, 3456], P('dp', 'grp')
- qkv_weight_new: float32 [1152, 3456], P('dp', 'grp')
- qkv_weight_mean_new: float32 [1152, 3456], P('dp', 'grp')
- qkv_weight_square_new: float32 [1152, 3456], P('dp', 'grp')
- proj_weight_grad: float32 [1152, 1152], P('dp', 'grp')
- proj_weight_new: float32 [1152, 1152], P('dp', 'grp')
- proj_weight_mean_new: float32 [1152, 1152], P('dp', 'grp')
- proj_weight_square_new: float32 [1152, 1152], P('dp', 'grp')
- up_weight_grad: float32 [1152, 4608], P('dp', 'grp')
- up_weight_new: float32 [1152, 4608], P('dp', 'grp')
- up_weight_mean_new: float32 [1152, 4608], P('dp', 'grp')
- up_weight_square_new: float32 [1152, 4608], P('dp', 'grp')
- down_weight_grad: float32 [4608, 1152], P('dp', 'grp')
- down_weight_new: float32 [4608, 1152], P('dp', 'grp')
- down_weight_mean_new: float32 [4608, 1152], P('dp', 'grp')
- down_weight_square_new: float32 [4608, 1152], P('dp', 'grp')
- main_bias_grad: float32 [9216], P(('dp', 'grp'))
- main_bias_new: float32 [9216], P(('dp', 'grp'))
- main_bias_mean_new: float32 [9216], P(('dp', 'grp'))
- main_bias_square_new: float32 [9216], P(('dp', 'grp'))
The draws below stay inside these ranges and needn't reach their ends.
Inputs may be any that keep to these rules, and one draw needn't show every extreme that they name: `slot_valid`: each index of dp has 2 slots; some index of dp has all 2 valid; exactly 24 slots are valid in all. `latent_of`: the valid slots name each of the 24 latents exactly once; a padding slot names some latent and is ignored.
All inputs are finite; a program needn't handle non-finite values.
Results may differ from the reference program's by a relative error of at most 0.024.
Values may be sent and summed in bfloat16 or wider, within the bound.
A program may use at most 256 MiB of HBM per device.

```python
import math
import jax
import jax.numpy as jnp
from jax import lax

D = 1152
HD = 72
HEADS = 16
FF = 4608
HW = 1152
LAT_TOK = 512
SLOTS = 2
ALL_SLOTS = 32
LATENTS = 24
BIAS_LEN = 9216


def slot_layout(key):
    folded = jax.random.fold_in(key, 4242)
    subkeys = jax.random.split(folded, 4)
    groups = ALL_SLOTS // SLOTS
    pattern = jnp.tile(jnp.array([2, 2, 1, 1], jnp.int32), groups // 4)
    counts = jax.random.permutation(subkeys[0], pattern)
    slot_order = jax.vmap(lambda subkey: jax.random.permutation(subkey, SLOTS))(jax.random.split(subkeys[1], groups))
    valid_flags = (slot_order < counts[:, None]).astype(jnp.int32).reshape(-1)
    valid_rank = jnp.cumsum(valid_flags) - valid_flags
    shuffled = jax.random.permutation(subkeys[2], LATENTS)
    filler = jax.random.randint(subkeys[3], (ALL_SLOTS,), 0, LATENTS)
    latent = jnp.where(valid_flags == 1, shuffled[jnp.minimum(valid_rank, LATENTS - 1)], filler)
    return (latent.astype(jnp.int32), valid_flags)


def draw_latent_of(key, part):
    return slot_layout(key)[0]


def draw_slot_valid(key, part):
    return slot_layout(key)[1]


def draw_up_weight(key, part):
    folded = jax.random.fold_in(key, 7171)
    noise_key, column_key = jax.random.split(folded)
    noise = jnp.clip(jax.random.normal(noise_key, (D, FF), jnp.float32), -6.0, 6.0)
    column = jnp.clip(jax.random.normal(column_key, (FF,), jnp.float32), -6.0, 6.0)
    return ((noise + 0.3 * column[None, :]) * (1.0 / math.sqrt(D))).astype(jnp.float32)


def level_of(stream_key, dims, shards, least, largest):
    def one(axis_at, shards_of):
        heights = jax.random.uniform(jax.random.fold_in(jax.random.fold_in(stream_key, 6), axis_at), (shards_of,), jnp.float32, least / len(shards), largest / len(shards))
        return jnp.repeat(jnp.exp(heights), dims[axis_at] // shards_of).reshape((-1,) + (1,) * (len(dims) - axis_at - 1))

    gain = one(*shards[0])
    for cut in shards[1:]:
        gain = gain * one(*cut)
    return gain


def scatter_about(own_key, shape, deviation, most, pieces=(), held_as=jnp.bfloat16):
    result = deviation * jax.random.normal(own_key, shape, jnp.float32)
    if pieces:
        result = result * level_of(own_key, shape, pieces, -0.22, 0.18)
    return jnp.clip(result, -most, most).astype(held_as)


def setup_inputs(seed: int = 0) -> dict:
    key_list = jax.random.split(jax.random.key(seed), 27)
    tokens = scatter_about(key_list[0], (ALL_SLOTS, LAT_TOK, D), 1.0, 6.0, ((0, 16), (1, 2)))
    cotangent = scatter_about(key_list[1], (ALL_SLOTS, LAT_TOK, D), 1.0, 6.0, ((0, 16), (1, 2)))
    condition = scatter_about(key_list[2], (LATENTS, D), 1.0, 6.0, ((1, 16),), jnp.float32)
    latent_of = draw_latent_of(jax.random.fold_in(key_list[26], 71), 0)
    slot_valid = draw_slot_valid(jax.random.fold_in(key_list[26], 71), 0)
    ada_weight = scatter_about(key_list[5], (D, 6 * D), D ** -0.5, 0.1875, ((0, 16), (1, 2)), jnp.float32)
    ada_weight_mean = scatter_about(key_list[6], (D, 6 * D), 0.002, 0.03125, ((0, 16), (1, 2)), jnp.float32)
    ada_weight_square = jnp.clip(jnp.exp(math.log(9.999999747378752e-06) - 1.609438 * jax.random.uniform(key_list[7], (D, 6 * D), jnp.float32) ** level_of(key_list[7], (D, 6 * D), ((0, 16), (1, 2)), -0.2, 0.2)), 1.9999999949504854e-06, 9.999999747378752e-06)
    ada_offset = scatter_about(key_list[8], (6 * D,), 0.05, 0.75, ((0, 2),), jnp.float32)
    ada_offset_mean = scatter_about(key_list[9], (6 * D,), 0.002, 0.03125, ((0, 2),), jnp.float32)
    ada_offset_square = jnp.clip(jnp.exp(math.log(9.999999747378752e-06) - 1.609438 * jax.random.uniform(key_list[10], (6 * D,), jnp.float32) ** level_of(key_list[10], (6 * D,), ((0, 2),), -0.2, 0.2)), 1.9999999949504854e-06, 9.999999747378752e-06)
    qkv_weight = scatter_about(key_list[11], (D, 3 * HW), D ** -0.5, 0.1875, ((0, 16), (1, 2)), jnp.float32)
    qkv_weight_mean = scatter_about(key_list[12], (D, 3 * HW), 0.002, 0.03125, ((0, 16), (1, 2)), jnp.float32)
    qkv_weight_square = jnp.clip(jnp.exp(math.log(9.999999747378752e-06) - 1.609438 * jax.random.uniform(key_list[13], (D, 3 * HW), jnp.float32) ** level_of(key_list[13], (D, 3 * HW), ((0, 16), (1, 2)), -0.2, 0.2)), 1.9999999949504854e-06, 9.999999747378752e-06)
    proj_weight = scatter_about(key_list[14], (HW, D), (HW // 8) ** -0.5, 0.5, ((0, 16), (1, 2)), jnp.float32)
    proj_weight_mean = scatter_about(key_list[15], (HW, D), 0.002, 0.03125, ((0, 16), (1, 2)), jnp.float32)
    proj_weight_square = jnp.clip(jnp.exp(math.log(9.999999747378752e-06) - 1.609438 * jax.random.uniform(key_list[16], (HW, D), jnp.float32) ** level_of(key_list[16], (HW, D), ((0, 16), (1, 2)), -0.2, 0.2)), 1.9999999949504854e-06, 9.999999747378752e-06)
    up_weight = draw_up_weight(jax.random.fold_in(key_list[26], 71), 0)
    up_weight_mean = scatter_about(key_list[18], (D, FF), 0.002, 0.03125, ((0, 16), (1, 2)), jnp.float32)
    up_weight_square = jnp.clip(jnp.exp(math.log(9.999999747378752e-06) - 1.609438 * jax.random.uniform(key_list[19], (D, FF), jnp.float32) ** level_of(key_list[19], (D, FF), ((0, 16), (1, 2)), -0.2, 0.2)), 1.9999999949504854e-06, 9.999999747378752e-06)
    down_weight = scatter_about(key_list[20], (FF, D), (D // 4) ** -0.5, 0.375, ((0, 16), (1, 2)), jnp.float32)
    down_weight_mean = scatter_about(key_list[21], (FF, D), 0.002, 0.03125, ((0, 16), (1, 2)), jnp.float32)
    down_weight_square = jnp.clip(jnp.exp(math.log(9.999999747378752e-06) - 1.609438 * jax.random.uniform(key_list[22], (FF, D), jnp.float32) ** level_of(key_list[22], (FF, D), ((0, 16), (1, 2)), -0.2, 0.2)), 1.9999999949504854e-06, 9.999999747378752e-06)
    main_bias = scatter_about(key_list[23], (BIAS_LEN,), 0.05, 0.75, ((0, 32),), jnp.float32)
    main_bias_mean = scatter_about(key_list[24], (BIAS_LEN,), 0.002, 0.03125, ((0, 32),), jnp.float32)
    main_bias_square = jnp.clip(jnp.exp(math.log(9.999999747378752e-06) - 1.609438 * jax.random.uniform(key_list[25], (BIAS_LEN,), jnp.float32) ** level_of(key_list[25], (BIAS_LEN,), ((0, 32),), -0.2, 0.2)), 1.9999999949504854e-06, 9.999999747378752e-06)
    return {"tokens": tokens, "cotangent": cotangent, "condition": condition, "latent_of": latent_of, "slot_valid": slot_valid, "ada_weight": ada_weight, "ada_weight_mean": ada_weight_mean, "ada_weight_square": ada_weight_square, "ada_offset": ada_offset, "ada_offset_mean": ada_offset_mean, "ada_offset_square": ada_offset_square, "qkv_weight": qkv_weight, "qkv_weight_mean": qkv_weight_mean, "qkv_weight_square": qkv_weight_square, "proj_weight": proj_weight, "proj_weight_mean": proj_weight_mean, "proj_weight_square": proj_weight_square, "up_weight": up_weight, "up_weight_mean": up_weight_mean, "up_weight_square": up_weight_square, "down_weight": down_weight, "down_weight_mean": down_weight_mean, "down_weight_square": down_weight_square, "main_bias": main_bias, "main_bias_mean": main_bias_mean, "main_bias_square": main_bias_square}


eps_norm = 1e-06
beta_one = 0.9
beta_two = 0.95
learn_rate = 0.015
decay_rate = 0.01
adam_eps = 1e-08
clip_rms = 0.01
clip_eps = 1e-06
step_count = 10
gelu_coef = 0.7978845608028654
cubic_term = 0.044715
highest = lax.Precision.HIGHEST

def product(left, right):
    return jnp.dot(left, right, preferred_element_type=jnp.float32)

def batched(pattern, left, right):
    return jnp.einsum(pattern, left.astype(jnp.float32), right.astype(jnp.float32))

def gelu_forward(values):
    inside = gelu_coef * (values + cubic_term * values * values * values)
    return 0.5 * values * (1.0 + jnp.tanh(inside))

def gelu_slope(values):
    inside = gelu_coef * (values + cubic_term * values * values * values)
    tangent = jnp.tanh(inside)
    return 0.5 * (1.0 + tangent) + 0.5 * values * (1.0 - tangent * tangent) * gelu_coef * (1.0 + 3.0 * cubic_term * values * values)

def layer_norm(values):
    centred = values - lax.optimization_barrier(jnp.mean(values, axis=-1, keepdims=True))
    inv_std = lax.rsqrt(lax.optimization_barrier(jnp.mean(centred * centred, axis=-1, keepdims=True)) + eps_norm)
    return (centred * inv_std, inv_std)

def norm_back(grad_normed, normed, inv_std):
    return inv_std * (grad_normed - lax.optimization_barrier(jnp.mean(grad_normed, axis=-1, keepdims=True)) - normed * lax.optimization_barrier(jnp.mean(grad_normed * normed, axis=-1, keepdims=True)))

def adam_update(weight, first_mom, second_mom, gradient, factor):
    clipped = gradient * factor
    first_new = beta_one * first_mom + (1.0 - beta_one) * clipped
    second_new = beta_two * second_mom + (1.0 - beta_two) * clipped * clipped
    corr_one = 1.0 - beta_one ** step_count
    corr_two = 1.0 - beta_two ** step_count
    direction = first_new / corr_one / (jnp.sqrt(second_new / corr_two) + adam_eps)
    weight_new = weight - learn_rate * (direction + decay_rate * weight)
    return (weight_new, first_new, second_new)

def clip_from(total, count):
    return jnp.minimum(1.0, clip_rms * lax.rsqrt(total / count + clip_eps))

def slot_pass(carried, inputs, qkv16, proj16, up16, down16, bias_float):
    qkv_acc, proj_acc, up_acc, down_acc, bias_acc = carried
    tokens_half, cot_half, mod_row, slot_keep = inputs
    shift_one = mod_row[:D]
    scale_one = mod_row[D:2 * D]
    gate_one = mod_row[2 * D:3 * D]
    shift_two = mod_row[3 * D:4 * D]
    scale_two = mod_row[4 * D:5 * D]
    gate_two = mod_row[5 * D:]
    bias_query = bias_float[:HW]
    bias_value = bias_float[HW:2 * HW]
    bias_proj = bias_float[2 * HW:2 * HW + D]
    bias_up = bias_float[2 * HW + D:2 * HW + D + FF]
    bias_down = bias_float[2 * HW + D + FF:]
    scale_dot = 1.0 / math.sqrt(HD)
    tok_float = tokens_half.astype(jnp.float32)
    normed_one, inv_one = layer_norm(tok_float)
    hidden_one = (normed_one * (1.0 + scale_one) + shift_one).astype(jnp.bfloat16)
    projected = product(hidden_one, qkv16)
    queries = (projected[:, :HW] + bias_query).astype(jnp.bfloat16)
    keys_all = projected[:, HW:2 * HW].astype(jnp.bfloat16)
    values_all = (projected[:, 2 * HW:] + bias_value).astype(jnp.bfloat16)
    query_heads = queries.reshape(LAT_TOK, HEADS, HD)
    key_heads = keys_all.reshape(LAT_TOK, HEADS, HD)
    value_heads = values_all.reshape(LAT_TOK, HEADS, HD)
    scores = batched('qhd,khd->hqk', query_heads, key_heads) * scale_dot
    row_max = lax.optimization_barrier(jnp.max(scores, axis=-1, keepdims=True))
    log_total = row_max + jnp.log(lax.optimization_barrier(jnp.sum(jnp.exp(scores - row_max), axis=-1, keepdims=True)))
    probs_half = jnp.exp(scores - log_total).astype(jnp.bfloat16)
    attended = batched('hqk,khd->qhd', probs_half, value_heads).reshape(LAT_TOK, HW).astype(jnp.bfloat16)
    branch = product(attended, proj16) + bias_proj
    mid_stream = tok_float + gate_one * branch
    normed_two, inv_two = layer_norm(mid_stream)
    hidden_two = (normed_two * (1.0 + scale_two) + shift_two).astype(jnp.bfloat16)
    up_pre = product(hidden_two, up16) + bias_up
    active = gelu_forward(up_pre).astype(jnp.bfloat16)
    mlp_out = product(active, down16) + bias_down
    block_out = ((mid_stream + gate_two * mlp_out) * slot_keep).astype(jnp.bfloat16)
    grad_out = cot_half.astype(jnp.float32) * slot_keep
    grad_gate_two = lax.optimization_barrier(jnp.sum(grad_out * mlp_out, axis=0))
    grad_mlp = grad_out * gate_two
    grad_mlp_half = grad_mlp.astype(jnp.bfloat16)
    down_acc = down_acc + product(active.T, grad_mlp_half)
    grad_up = product(grad_mlp_half, down16.T) * gelu_slope(up_pre)
    grad_up_half = grad_up.astype(jnp.bfloat16)
    up_acc = up_acc + product(hidden_two.T, grad_up_half)
    grad_hidden_two = product(grad_up_half, up16.T)
    grad_shift_two = lax.optimization_barrier(jnp.sum(grad_hidden_two, axis=0))
    grad_scale_two = lax.optimization_barrier(jnp.sum(grad_hidden_two * normed_two, axis=0))
    grad_mid = grad_out + norm_back(grad_hidden_two * (1.0 + scale_two), normed_two, inv_two)
    grad_gate_one = lax.optimization_barrier(jnp.sum(grad_mid * branch, axis=0))
    grad_branch = grad_mid * gate_one
    grad_branch_half = grad_branch.astype(jnp.bfloat16)
    grad_attended = product(grad_branch_half, proj16.T).astype(jnp.bfloat16)
    proj_acc = proj_acc + product(attended.T, grad_branch_half)
    grad_heads = grad_attended.reshape(LAT_TOK, HEADS, HD)
    out_heads = attended.reshape(LAT_TOK, HEADS, HD)
    row_delta = lax.optimization_barrier(jnp.sum(grad_heads.astype(jnp.float32) * out_heads.astype(jnp.float32), axis=-1)).T[:, :, None]
    scores_again = batched('qhd,khd->hqk', query_heads, key_heads) * scale_dot
    probs_float = jnp.exp(scores_again - log_total)
    grad_probs = batched('qhd,khd->hqk', grad_heads, value_heads)
    grad_scores = (probs_float * (grad_probs - row_delta) * scale_dot).astype(jnp.bfloat16)
    grad_query = batched('hqk,khd->qhd', grad_scores, key_heads).reshape(LAT_TOK, HW)
    grad_key = batched('hqk,qhd->khd', grad_scores, query_heads).reshape(LAT_TOK, HW)
    probs_again = probs_float.astype(jnp.bfloat16)
    grad_value = batched('hqk,qhd->khd', probs_again, grad_heads).reshape(LAT_TOK, HW)
    grad_qkv = jnp.concatenate([grad_query, grad_key, grad_value], axis=-1).astype(jnp.bfloat16)
    qkv_acc = qkv_acc + product(hidden_one.T, grad_qkv)
    bias_acc = bias_acc + jnp.concatenate([lax.optimization_barrier(jnp.sum(grad_query, axis=0)), lax.optimization_barrier(jnp.sum(grad_value, axis=0)), lax.optimization_barrier(jnp.sum(grad_branch, axis=0)), lax.optimization_barrier(jnp.sum(grad_up, axis=0)), lax.optimization_barrier(jnp.sum(grad_mlp, axis=0))])
    grad_hidden_one = product(grad_qkv, qkv16.T)
    grad_shift_one = lax.optimization_barrier(jnp.sum(grad_hidden_one, axis=0))
    grad_scale_one = lax.optimization_barrier(jnp.sum(grad_hidden_one * normed_one, axis=0))
    tokens_grad = (grad_mid + norm_back(grad_hidden_one * (1.0 + scale_one), normed_one, inv_one)).astype(jnp.bfloat16)
    mod_grad = jnp.concatenate([grad_shift_one, grad_scale_one, grad_gate_one, grad_shift_two, grad_scale_two, grad_gate_two])
    return ((qkv_acc, proj_acc, up_acc, down_acc, bias_acc), (block_out, tokens_grad, mod_grad))

def reference(tokens, cotangent, condition, latent_of, slot_valid, ada_weight, ada_weight_mean, ada_weight_square, ada_offset, ada_offset_mean, ada_offset_square, qkv_weight, qkv_weight_mean, qkv_weight_square, proj_weight, proj_weight_mean, proj_weight_square, up_weight, up_weight_mean, up_weight_square, down_weight, down_weight_mean, down_weight_square, main_bias, main_bias_mean, main_bias_square):
    qkv16 = qkv_weight.astype(jnp.bfloat16)
    proj16 = proj_weight.astype(jnp.bfloat16)
    up16 = up_weight.astype(jnp.bfloat16)
    down16 = down_weight.astype(jnp.bfloat16)
    bias16 = lax.optimization_barrier(main_bias.astype(jnp.bfloat16))
    bias_float = bias16.astype(jnp.float32)
    silu_cond = jax.nn.silu(condition)
    mod_table = jnp.dot(silu_cond, ada_weight, precision=highest) + ada_offset
    slot_mod = mod_table[latent_of]
    slot_keep = slot_valid.astype(jnp.float32)

    def step_fn(carried, inputs):
        return slot_pass(carried, inputs, qkv16, proj16, up16, down16, bias_float)
    start_state = (jnp.zeros((D, 3 * HW), jnp.float32), jnp.zeros((HW, D), jnp.float32), jnp.zeros((D, FF), jnp.float32), jnp.zeros((FF, D), jnp.float32), jnp.zeros((2 * HW + 2 * D + FF,), jnp.float32))
    carried, stacked = lax.scan(step_fn, start_state, (tokens, cotangent, slot_mod, slot_keep))
    qkv_weight_grad, proj_weight_grad, up_weight_grad, down_weight_grad, main_bias_grad = carried
    block_out, tokens_grad, slot_mod_grad = stacked
    mod_grad = jnp.zeros((LATENTS, 6 * D), jnp.float32).at[latent_of].add(slot_mod_grad)
    ada_weight_grad = jnp.dot(silu_cond.T, mod_grad, precision=highest)
    ada_offset_grad = lax.optimization_barrier(jnp.sum(mod_grad, axis=0))
    sigmoid_cond = jax.nn.sigmoid(condition)
    condition_grad = jnp.dot(mod_grad, ada_weight.T, precision=highest) * sigmoid_cond * (1.0 + condition * (1.0 - sigmoid_cond))
    results = []
    for weight, first_mom, second_mom, gradient in ((ada_weight, ada_weight_mean, ada_weight_square, ada_weight_grad), (ada_offset, ada_offset_mean, ada_offset_square, ada_offset_grad), (qkv_weight, qkv_weight_mean, qkv_weight_square, qkv_weight_grad), (proj_weight, proj_weight_mean, proj_weight_square, proj_weight_grad), (up_weight, up_weight_mean, up_weight_square, up_weight_grad), (down_weight, down_weight_mean, down_weight_square, down_weight_grad), (main_bias, main_bias_mean, main_bias_square, main_bias_grad)):
        factor = clip_from(jnp.sum(gradient * gradient), gradient.size)
        weight_new, first_new, second_new = adam_update(weight, first_mom, second_mom, gradient, factor)
        results.append((gradient, weight_new, first_new, second_new))
    return (block_out, tokens_grad, condition_grad, results[0][0], results[0][1], results[0][2], results[0][3], results[1][0], results[1][1], results[1][2], results[1][3], results[2][0], results[2][1], results[2][2], results[2][3], results[3][0], results[3][1], results[3][2], results[3][3], results[4][0], results[4][1], results[4][2], results[4][3], results[5][0], results[5][1], results[5][2], results[5][3], results[6][0], results[6][1], results[6][2], results[6][3])
```

```python
import math

import jax
import jax.numpy as jnp
from jax import lax
from jax.sharding import PartitionSpec as P

D = 1152
HD = 72
HEADS = 16
FF = 4608
HW = 1152


eps_norm = 1e-06
beta_one = 0.9
beta_two = 0.95
learn_rate = 0.015
decay_rate = 0.01
adam_eps = 1e-08
clip_rms = 0.01
clip_eps = 1e-06
step_count = 10
gelu_coef = 0.7978845608028654
cubic_term = 0.044715
highest = lax.Precision.HIGHEST


def contract(pattern, left, right):
    return jnp.einsum(pattern, left, right, preferred_element_type=jnp.float32)


def gelu_forward(values):
    inside = gelu_coef * (values + cubic_term * values * values * values)
    return 0.5 * values * (1.0 + jnp.tanh(inside))


def gelu_slope(values):
    inside = gelu_coef * (values + cubic_term * values * values * values)
    tangent = jnp.tanh(inside)
    return 0.5 * (1.0 + tangent) + 0.5 * values * (1.0 - tangent * tangent) * gelu_coef * (
        1.0 + 3.0 * cubic_term * values * values
    )


def layer_norm(values):
    centred = values - jnp.mean(values, axis=-1, keepdims=True)
    inv_std = lax.rsqrt(jnp.mean(centred * centred, axis=-1, keepdims=True) + eps_norm)
    return (centred * inv_std, inv_std)


def norm_back(grad_normed, normed, inv_std):
    return inv_std * (
        grad_normed
        - jnp.mean(grad_normed, axis=-1, keepdims=True)
        - normed * jnp.mean(grad_normed * normed, axis=-1, keepdims=True)
    )


def adam_update(weight, first_mom, second_mom, gradient, factor):
    clipped = gradient * factor
    first_new = beta_one * first_mom + (1.0 - beta_one) * clipped
    second_new = beta_two * second_mom + (1.0 - beta_two) * clipped * clipped
    corr_one = 1.0 - beta_one**step_count
    corr_two = 1.0 - beta_two**step_count
    direction = first_new / corr_one / (jnp.sqrt(second_new / corr_two) + adam_eps)
    weight_new = weight - learn_rate * (direction + decay_rate * weight)
    return (weight_new, first_new, second_new)


def clip_from(total, count):
    return jnp.minimum(1.0, clip_rms * lax.rsqrt(total / count + clip_eps))


def split_heads(values):
    return values.reshape(values.shape[:-1] + (HEADS, HD))


def swap(values):
    return lax.ppermute(values, "grp", [(0, 1), (1, 0)])


ACROSS = (3, 2, 0, 1)
ALONG = (3, 2, 1, 0)


def data_bit(bit):
    return lax.rem(lax.axis_index("dp") // 2**bit, 2) == 1


def trade(values, bit):
    size = lax.axis_size("dp")
    return lax.ppermute(values, "dp", [(at, at ^ 2**bit) for at in range(size)])


def gather_data(values, order):
    shape = values.shape
    held = []
    for bit in order:
        other = trade(values, bit)
        upper = data_bit(bit)
        place = sum(have > bit for have in held)
        values = jnp.stack(
            [jnp.where(upper, other, values), jnp.where(upper, values, other)], axis=place
        )
        held.append(bit)
    return values.reshape((-1,) + shape[1:])


def scatter_data(values, order, wire):
    rows = values.shape[0] // lax.axis_size("dp")
    left = sorted(order, reverse=True)
    shape = (rows,) + values.shape[1:]
    values = values.reshape((2,) * len(left) + shape)
    for bit in reversed(order):
        place = left.index(bit)
        low = lax.index_in_dim(values, 0, place, keepdims=False)
        high = lax.index_in_dim(values, 1, place, keepdims=False)
        upper = data_bit(bit)
        kept = jnp.where(upper, high, low)
        sent = jnp.where(upper, low, high).astype(wire)
        values = kept + trade(sent, bit).astype(jnp.float32)
        left.remove(bit)
    return values


def total_over_all(values):
    for bit in ALONG:
        values = values + trade(values, bit)
    return values + swap(values)


def natural(own, other):
    first = lax.axis_index("grp") == 0
    return jnp.concatenate(
        [jnp.where(first, own, other), jnp.where(first, other, own)], axis=-1
    )


def cut(values):
    half = values.shape[-1] // 2
    first = lax.axis_index("grp") == 0
    low, high = values[..., :half], values[..., half:]
    return jnp.where(first, low, high), jnp.where(first, high, low)


def weight_halves(weight, order):
    own = gather_data(weight.astype(jnp.bfloat16), order)
    return own, swap(own)


def weight_grad(own, other, order):
    arrived = swap(other.astype(jnp.bfloat16))
    return scatter_data(own + arrived.astype(jnp.float32), order, jnp.bfloat16)


def local(
    tokens,
    cotangent,
    condition,
    latent_of,
    slot_valid,
    ada_weight,
    ada_weight_mean,
    ada_weight_square,
    ada_offset,
    ada_offset_mean,
    ada_offset_square,
    qkv_weight,
    qkv_weight_mean,
    qkv_weight_square,
    proj_weight,
    proj_weight_mean,
    proj_weight_square,
    up_weight,
    up_weight_mean,
    up_weight_square,
    down_weight,
    down_weight_mean,
    down_weight_square,
    main_bias,
    main_bias_mean,
    main_bias_square,
):
    latents = condition.shape[0]
    slot_count = tokens.shape[0]
    scale_dot = 1.0 / math.sqrt(HD)
    data_count = lax.axis_size("dp")
    data_at = lax.axis_index("dp")
    bias_share = main_bias.shape[0]
    packed = jnp.concatenate(
        [main_bias.astype(jnp.bfloat16).astype(jnp.float32), latent_of.astype(jnp.float32)]
    )
    packed_all = gather_data(packed[None], ALONG)
    packed_other = swap(packed_all)
    slots_named = packed_all[:, bias_share:].reshape(-1).astype(jnp.int32)
    bias_float = natural(packed_all[:, :bias_share], packed_other[:, :bias_share]).reshape(-1)
    bias_query = bias_float[:HW]
    bias_value = bias_float[HW : 2 * HW]
    bias_proj = bias_float[2 * HW : 2 * HW + D]
    bias_up = bias_float[2 * HW + D : 2 * HW + D + FF]
    bias_down = bias_float[2 * HW + D + FF :]
    silu_cond = jax.nn.silu(condition)
    first_data = jnp.where(data_at == 0, 1.0, 0.0).astype(jnp.float32)
    mod_piece = jnp.dot(silu_cond, ada_weight, precision=highest) + first_data * ada_offset
    all_pick = (slots_named[:, None] == jnp.arange(latents, dtype=jnp.int32)[None, :]).astype(
        jnp.float32
    )
    slot_piece = jnp.dot(all_pick, mod_piece, precision=highest)
    mod_own = scatter_data(slot_piece, ALONG, jnp.float32)
    slot_mod = natural(mod_own, swap(mod_own))[:, None, :]
    qkv_own, qkv_other = weight_halves(qkv_weight, ALONG)
    proj_own, proj_other = weight_halves(proj_weight, ACROSS)
    up_own, up_other = weight_halves(up_weight, ACROSS)
    down_own, down_other = weight_halves(down_weight, ALONG)
    shift_one = slot_mod[..., :D]
    scale_one = slot_mod[..., D : 2 * D]
    gate_one = slot_mod[..., 2 * D : 3 * D]
    shift_two = slot_mod[..., 3 * D : 4 * D]
    scale_two = slot_mod[..., 4 * D : 5 * D]
    gate_two = slot_mod[..., 5 * D :]
    slot_keep = slot_valid.astype(jnp.float32)[:, None, None]
    tok_float = tokens.astype(jnp.float32)
    normed_one, inv_one = layer_norm(tok_float)
    hidden_one = (normed_one * (1.0 + scale_one) + shift_one).astype(jnp.bfloat16)
    projected = natural(
        contract("std,de->ste", hidden_one, qkv_own), contract("std,de->ste", hidden_one, qkv_other)
    )
    queries = (projected[..., :HW] + bias_query).astype(jnp.bfloat16)
    keys_own = projected[..., HW : 2 * HW].astype(jnp.bfloat16)
    values_own = (projected[..., 2 * HW :] + bias_value).astype(jnp.bfloat16)
    own_tokens = keys_own.shape[1]
    keys_all = jnp.concatenate([keys_own, swap(keys_own)], axis=1)
    values_all = jnp.concatenate([values_own, swap(values_own)], axis=1)
    query_heads = split_heads(queries)
    key_heads = split_heads(keys_all)
    value_heads = split_heads(values_all)
    scores = contract("sqhd,skhd->shqk", query_heads, key_heads) * scale_dot
    row_max = jnp.max(scores, axis=-1, keepdims=True)
    log_total = row_max + jnp.log(jnp.sum(jnp.exp(scores - row_max), axis=-1, keepdims=True))
    probs_half = jnp.exp(scores - log_total).astype(jnp.bfloat16)
    attended = (
        contract("shqk,skhd->sqhd", probs_half, value_heads)
        .astype(jnp.bfloat16)
        .reshape(queries.shape)
    )
    branch = (
        natural(
            contract("ste,ed->std", attended, proj_own),
            contract("ste,ed->std", attended, proj_other),
        )
        + bias_proj
    )
    mid_stream = tok_float + gate_one * branch
    normed_two, inv_two = layer_norm(mid_stream)
    hidden_two = (normed_two * (1.0 + scale_two) + shift_two).astype(jnp.bfloat16)
    up_pre = (
        natural(
            contract("std,df->stf", hidden_two, up_own),
            contract("std,df->stf", hidden_two, up_other),
        )
        + bias_up
    )
    active = gelu_forward(up_pre).astype(jnp.bfloat16)
    mlp_out = (
        natural(
            contract("stf,fd->std", active, down_own), contract("stf,fd->std", active, down_other)
        )
        + bias_down
    )
    block_out = ((mid_stream + gate_two * mlp_out) * slot_keep).astype(jnp.bfloat16)
    grad_out = cotangent.astype(jnp.float32) * slot_keep
    grad_gate_two = jnp.sum(grad_out * mlp_out, axis=1)
    grad_mlp = grad_out * gate_two
    grad_mlp_half = grad_mlp.astype(jnp.bfloat16)
    mlp_own, mlp_other = cut(grad_mlp_half)
    down_weight_grad = weight_grad(
        contract("stf,std->fd", active, mlp_own),
        contract("stf,std->fd", active, mlp_other),
        ALONG,
    )
    grad_up = (
        contract("std,fd->stf", mlp_own, down_own) + contract("std,fd->stf", mlp_other, down_other)
    ) * gelu_slope(up_pre)
    grad_up_half = grad_up.astype(jnp.bfloat16)
    rise_own, rise_other = cut(grad_up_half)
    up_weight_grad = weight_grad(
        contract("std,stf->df", hidden_two, rise_own),
        contract("std,stf->df", hidden_two, rise_other),
        ACROSS,
    )
    grad_hidden_two = contract("stf,df->std", rise_own, up_own) + contract(
        "stf,df->std", rise_other, up_other
    )
    grad_shift_two = jnp.sum(grad_hidden_two, axis=1)
    grad_scale_two = jnp.sum(grad_hidden_two * normed_two, axis=1)
    grad_mid = grad_out + norm_back(grad_hidden_two * (1.0 + scale_two), normed_two, inv_two)
    grad_gate_one = jnp.sum(grad_mid * branch, axis=1)
    grad_branch = grad_mid * gate_one
    grad_branch_half = grad_branch.astype(jnp.bfloat16)
    fork_own, fork_other = cut(grad_branch_half)
    grad_attended = (
        contract("std,ed->ste", fork_own, proj_own) + contract("std,ed->ste", fork_other, proj_other)
    ).astype(jnp.bfloat16)
    proj_weight_grad = weight_grad(
        contract("ste,std->ed", attended, fork_own),
        contract("ste,std->ed", attended, fork_other),
        ACROSS,
    )
    grad_heads = split_heads(grad_attended)
    out_heads = split_heads(attended)
    row_delta = jnp.transpose(
        jnp.sum(grad_heads.astype(jnp.float32) * out_heads.astype(jnp.float32), axis=-1), (0, 2, 1)
    )[..., None]
    scores_again = contract("sqhd,skhd->shqk", query_heads, key_heads) * scale_dot
    probs_float = jnp.exp(scores_again - log_total)
    grad_probs = contract("sqhd,skhd->shqk", grad_heads, value_heads)
    grad_scores = (probs_float * (grad_probs - row_delta) * scale_dot).astype(jnp.bfloat16)
    grad_query = contract("shqk,skhd->sqhd", grad_scores, key_heads).reshape(queries.shape)
    key_partial = contract("shqk,sqhd->skhd", grad_scores, query_heads).reshape(keys_all.shape)
    value_partial = contract(
        "shqk,sqhd->skhd", probs_float.astype(jnp.bfloat16), grad_heads
    ).reshape(values_all.shape)
    grad_key = key_partial[:, :own_tokens] + swap(
        key_partial[:, own_tokens:].astype(jnp.bfloat16)
    ).astype(jnp.float32)
    grad_value = value_partial[:, :own_tokens] + swap(
        value_partial[:, own_tokens:].astype(jnp.bfloat16)
    ).astype(jnp.float32)
    grad_qkv = jnp.concatenate([grad_query, grad_key, grad_value], axis=-1).astype(jnp.bfloat16)
    trio_own, trio_other = cut(grad_qkv)
    qkv_weight_grad = weight_grad(
        contract("std,ste->de", hidden_one, trio_own),
        contract("std,ste->de", hidden_one, trio_other),
        ALONG,
    )
    bias_local = jnp.concatenate(
        [
            jnp.sum(grad_query, axis=(0, 1)),
            jnp.sum(grad_value, axis=(0, 1)),
            jnp.sum(grad_branch, axis=(0, 1)),
            jnp.sum(grad_up, axis=(0, 1)),
            jnp.sum(grad_mlp, axis=(0, 1)),
        ]
    ).reshape(data_count, -1)
    grad_hidden_one = contract("ste,de->std", trio_own, qkv_own) + contract(
        "ste,de->std", trio_other, qkv_other
    )
    grad_shift_one = jnp.sum(grad_hidden_one, axis=1)
    grad_scale_one = jnp.sum(grad_hidden_one * normed_one, axis=1)
    tokens_grad = (
        grad_mid + norm_back(grad_hidden_one * (1.0 + scale_one), normed_one, inv_one)
    ).astype(jnp.bfloat16)
    slot_mod_grad = jnp.concatenate(
        [
            grad_shift_one,
            grad_scale_one,
            grad_gate_one,
            grad_shift_two,
            grad_scale_two,
            grad_gate_two,
        ],
        axis=-1,
    )
    bias_own, bias_other = cut(bias_local)
    mod_grad_own, mod_grad_other = cut(slot_mod_grad)
    bias_entries = bias_own.size
    vector_own = jnp.concatenate([bias_own.reshape(-1), mod_grad_own.reshape(-1)])
    vector_other = jnp.concatenate([bias_other.reshape(-1), mod_grad_other.reshape(-1)])
    vectors = gather_data((vector_own + swap(vector_other))[None], ALONG)
    main_bias_grad = jnp.sum(
        lax.dynamic_slice_in_dim(
            vectors[:, :bias_entries].reshape(data_count, data_count, -1), data_at, 1, 1
        ),
        axis=(0, 1),
    )
    slot_rows = vectors[:, bias_entries:].reshape(data_count * slot_count, -1)
    mod_grad_cols = jnp.dot(all_pick.T, slot_rows, precision=highest)
    ada_weight_grad = jnp.dot(silu_cond.T, mod_grad_cols, precision=highest)
    ada_offset_grad = jnp.sum(mod_grad_cols, axis=0)
    cond_partial = jnp.dot(mod_grad_cols, ada_weight.T, precision=highest)
    cond_total = cond_partial + swap(cond_partial)
    sigmoid_cond = jax.nn.sigmoid(condition)
    condition_grad = cond_total * sigmoid_cond * (1.0 + condition * (1.0 - sigmoid_cond))
    square_sums = total_over_all(
        jnp.stack(
            [
                jnp.sum(ada_weight_grad * ada_weight_grad),
                jnp.sum(ada_offset_grad * ada_offset_grad) / data_count,
                jnp.sum(qkv_weight_grad * qkv_weight_grad),
                jnp.sum(proj_weight_grad * proj_weight_grad),
                jnp.sum(up_weight_grad * up_weight_grad),
                jnp.sum(down_weight_grad * down_weight_grad),
                jnp.sum(main_bias_grad * main_bias_grad),
            ]
        )
    )
    entry_counts = (D * 6 * D, 6 * D, D * 3 * HW, HW * D, D * FF, FF * D, 2 * HW + 2 * D + FF)
    results = []
    for index_param, (weight, first_mom, second_mom, gradient) in enumerate(
        (
            (ada_weight, ada_weight_mean, ada_weight_square, ada_weight_grad),
            (ada_offset, ada_offset_mean, ada_offset_square, ada_offset_grad),
            (qkv_weight, qkv_weight_mean, qkv_weight_square, qkv_weight_grad),
            (proj_weight, proj_weight_mean, proj_weight_square, proj_weight_grad),
            (up_weight, up_weight_mean, up_weight_square, up_weight_grad),
            (down_weight, down_weight_mean, down_weight_square, down_weight_grad),
            (main_bias, main_bias_mean, main_bias_square, main_bias_grad),
        )
    ):
        factor = clip_from(square_sums[index_param], entry_counts[index_param])
        weight_new, first_new, second_new = adam_update(
            weight, first_mom, second_mom, gradient, factor
        )
        results.append((gradient, weight_new, first_new, second_new))
    return (
        block_out,
        tokens_grad,
        condition_grad,
        results[0][0],
        results[0][1],
        results[0][2],
        results[0][3],
        results[1][0],
        results[1][1],
        results[1][2],
        results[1][3],
        results[2][0],
        results[2][1],
        results[2][2],
        results[2][3],
        results[3][0],
        results[3][1],
        results[3][2],
        results[3][3],
        results[4][0],
        results[4][1],
        results[4][2],
        results[4][3],
        results[5][0],
        results[5][1],
        results[5][2],
        results[5][3],
        results[6][0],
        results[6][1],
        results[6][2],
        results[6][3],
    )


def reduce_bucket(first_grad, second_grad, bias_grad):
    bias_rows = bias_grad.reshape(lax.axis_size("dp"), -1)
    summed = (
        lax.psum_scatter(
            first_grad.astype(jnp.bfloat16), "dp", scatter_dimension=0, tiled=True
        ).astype(jnp.float32),
        lax.psum_scatter(
            second_grad.astype(jnp.bfloat16), "dp", scatter_dimension=0, tiled=True
        ).astype(jnp.float32),
        lax.psum_scatter(
            bias_rows.astype(jnp.bfloat16), "dp", scatter_dimension=0, tiled=True
        ).astype(jnp.float32),
    )
    owned = (
        lax.psum_scatter(
            summed[0].astype(jnp.bfloat16), "grp", scatter_dimension=1, tiled=True
        ).astype(jnp.float32),
        lax.psum_scatter(
            summed[1].astype(jnp.bfloat16), "grp", scatter_dimension=1, tiled=True
        ).astype(jnp.float32),
        lax.psum_scatter(
            summed[2].astype(jnp.bfloat16), "grp", scatter_dimension=1, tiled=True
        ).astype(jnp.float32),
    )
    return (owned[0], owned[1], owned[2].reshape(-1))


def local_general(
    tokens,
    cotangent,
    condition,
    latent_of,
    slot_valid,
    ada_weight,
    ada_weight_mean,
    ada_weight_square,
    ada_offset,
    ada_offset_mean,
    ada_offset_square,
    qkv_weight,
    qkv_weight_mean,
    qkv_weight_square,
    proj_weight,
    proj_weight_mean,
    proj_weight_square,
    up_weight,
    up_weight_mean,
    up_weight_square,
    down_weight,
    down_weight_mean,
    down_weight_square,
    main_bias,
    main_bias_mean,
    main_bias_square,
):
    latents = condition.shape[0]
    slot_count = tokens.shape[0]
    scale_dot = 1.0 / math.sqrt(HD)
    qkv_part, proj_part, up_part, down_part, bias_part = (
        lax.all_gather(qkv_weight.astype(jnp.bfloat16), "grp", axis=1, tiled=True),
        lax.all_gather(proj_weight.astype(jnp.bfloat16), "grp", axis=1, tiled=True),
        lax.all_gather(up_weight.astype(jnp.bfloat16), "grp", axis=1, tiled=True),
        lax.all_gather(down_weight.astype(jnp.bfloat16), "grp", axis=1, tiled=True),
        lax.all_gather(main_bias.astype(jnp.bfloat16), "grp", axis=0, tiled=True),
    )
    qkv_full, proj_full, up_full, down_full, bias_full = (
        lax.all_gather(qkv_part, "dp", axis=0, tiled=True),
        lax.all_gather(proj_part, "dp", axis=0, tiled=True),
        lax.all_gather(up_part, "dp", axis=0, tiled=True),
        lax.all_gather(down_part, "dp", axis=0, tiled=True),
        lax.all_gather(bias_part, "dp", axis=0, tiled=True),
    )
    bias_float = bias_full.astype(jnp.float32)
    bias_query = bias_float[:HW]
    bias_value = bias_float[HW : 2 * HW]
    bias_proj = bias_float[2 * HW : 2 * HW + D]
    bias_up = bias_float[2 * HW + D : 2 * HW + D + FF]
    bias_down = bias_float[2 * HW + D + FF :]
    silu_cond = jax.nn.silu(condition)
    col_width = ada_weight.shape[1]
    first_data = jnp.where(lax.axis_index("dp") == 0, 1.0, 0.0).astype(jnp.float32)
    mod_piece = jnp.dot(silu_cond, ada_weight, precision=highest) + first_data * ada_offset
    mod_spread = lax.dynamic_update_slice_in_dim(
        jnp.zeros((latents, 6 * D), jnp.float32), mod_piece, lax.axis_index("grp") * col_width, 1
    )
    mod_table = lax.psum(mod_spread, ("dp", "grp"))
    slot_pick = (latent_of[:, None] == jnp.arange(latents, dtype=jnp.int32)[None, :]).astype(
        jnp.float32
    )
    slot_mod = jnp.dot(slot_pick, mod_table, precision=highest)[:, None, :]
    shift_one = slot_mod[..., :D]
    scale_one = slot_mod[..., D : 2 * D]
    gate_one = slot_mod[..., 2 * D : 3 * D]
    shift_two = slot_mod[..., 3 * D : 4 * D]
    scale_two = slot_mod[..., 4 * D : 5 * D]
    gate_two = slot_mod[..., 5 * D :]
    slot_keep = slot_valid.astype(jnp.float32)[:, None, None]
    tok_float = tokens.astype(jnp.float32)
    normed_one, inv_one = layer_norm(tok_float)
    hidden_one = (normed_one * (1.0 + scale_one) + shift_one).astype(jnp.bfloat16)
    projected = contract("std,de->ste", hidden_one, qkv_full)
    queries = (projected[..., :HW] + bias_query).astype(jnp.bfloat16)
    keys_own = projected[..., HW : 2 * HW].astype(jnp.bfloat16)
    values_own = (projected[..., 2 * HW :] + bias_value).astype(jnp.bfloat16)
    keys_all, values_all = (
        lax.all_gather(keys_own, "grp", axis=1, tiled=True),
        lax.all_gather(values_own, "grp", axis=1, tiled=True),
    )
    query_heads = split_heads(queries)
    key_heads = split_heads(keys_all)
    value_heads = split_heads(values_all)
    scores = contract("sqhd,skhd->shqk", query_heads, key_heads) * scale_dot
    row_max = jnp.max(scores, axis=-1, keepdims=True)
    log_total = row_max + jnp.log(jnp.sum(jnp.exp(scores - row_max), axis=-1, keepdims=True))
    probs_half = jnp.exp(scores - log_total).astype(jnp.bfloat16)
    attended = (
        contract("shqk,skhd->sqhd", probs_half, value_heads)
        .astype(jnp.bfloat16)
        .reshape(queries.shape)
    )
    branch = contract("ste,ed->std", attended, proj_full) + bias_proj
    mid_stream = tok_float + gate_one * branch
    normed_two, inv_two = layer_norm(mid_stream)
    hidden_two = (normed_two * (1.0 + scale_two) + shift_two).astype(jnp.bfloat16)
    up_pre = contract("std,df->stf", hidden_two, up_full) + bias_up
    active = gelu_forward(up_pre).astype(jnp.bfloat16)
    mlp_out = contract("stf,fd->std", active, down_full) + bias_down
    block_out = ((mid_stream + gate_two * mlp_out) * slot_keep).astype(jnp.bfloat16)
    grad_out = cotangent.astype(jnp.float32) * slot_keep
    grad_gate_two = jnp.sum(grad_out * mlp_out, axis=1)
    grad_mlp = grad_out * gate_two
    grad_mlp_half = grad_mlp.astype(jnp.bfloat16)
    down_local = contract("stf,std->fd", active, grad_mlp_half)
    grad_up = contract("std,fd->stf", grad_mlp_half, down_full) * gelu_slope(up_pre)
    grad_up_half = grad_up.astype(jnp.bfloat16)
    up_local = contract("std,stf->df", hidden_two, grad_up_half)
    mlp_bias_local = jnp.concatenate(
        [
            jnp.zeros((2 * HW + D,), jnp.float32),
            jnp.sum(grad_up, axis=(0, 1)),
            jnp.sum(grad_mlp, axis=(0, 1)),
        ]
    )
    up_weight_grad, down_weight_grad, mlp_bias_grad = reduce_bucket(
        up_local, down_local, mlp_bias_local
    )
    grad_hidden_two = contract("stf,df->std", grad_up_half, up_full)
    grad_shift_two = jnp.sum(grad_hidden_two, axis=1)
    grad_scale_two = jnp.sum(grad_hidden_two * normed_two, axis=1)
    grad_mid = grad_out + norm_back(grad_hidden_two * (1.0 + scale_two), normed_two, inv_two)
    grad_gate_one = jnp.sum(grad_mid * branch, axis=1)
    grad_branch = grad_mid * gate_one
    grad_branch_half = grad_branch.astype(jnp.bfloat16)
    grad_attended = contract("std,ed->ste", grad_branch_half, proj_full).astype(jnp.bfloat16)
    proj_local = contract("ste,std->ed", attended, grad_branch_half)
    grad_heads = split_heads(grad_attended)
    out_heads = split_heads(attended)
    row_delta = jnp.transpose(
        jnp.sum(grad_heads.astype(jnp.float32) * out_heads.astype(jnp.float32), axis=-1), (0, 2, 1)
    )[..., None]
    scores_again = contract("sqhd,skhd->shqk", query_heads, key_heads) * scale_dot
    probs_float = jnp.exp(scores_again - log_total)
    grad_probs = contract("sqhd,skhd->shqk", grad_heads, value_heads)
    grad_scores = (probs_float * (grad_probs - row_delta) * scale_dot).astype(jnp.bfloat16)
    grad_query = contract("shqk,skhd->sqhd", grad_scores, key_heads).reshape(queries.shape)
    key_partial = contract("shqk,sqhd->skhd", grad_scores, query_heads).reshape(keys_all.shape)
    value_partial = contract(
        "shqk,sqhd->skhd", probs_float.astype(jnp.bfloat16), grad_heads
    ).reshape(values_all.shape)
    grad_key, grad_value = (
        lax.psum_scatter(
            key_partial.astype(jnp.bfloat16), "grp", scatter_dimension=1, tiled=True
        ).astype(jnp.float32),
        lax.psum_scatter(
            value_partial.astype(jnp.bfloat16), "grp", scatter_dimension=1, tiled=True
        ).astype(jnp.float32),
    )
    grad_qkv = jnp.concatenate([grad_query, grad_key, grad_value], axis=-1).astype(jnp.bfloat16)
    qkv_local = contract("std,ste->de", hidden_one, grad_qkv)
    attn_bias_local = jnp.concatenate(
        [
            jnp.sum(grad_query, axis=(0, 1)),
            jnp.sum(grad_value, axis=(0, 1)),
            jnp.sum(grad_branch, axis=(0, 1)),
            jnp.zeros((FF + D,), jnp.float32),
        ]
    )
    qkv_weight_grad, proj_weight_grad, attn_bias_grad = reduce_bucket(
        qkv_local, proj_local, attn_bias_local
    )
    main_bias_grad = mlp_bias_grad + attn_bias_grad
    grad_hidden_one = contract("ste,de->std", grad_qkv, qkv_full)
    grad_shift_one = jnp.sum(grad_hidden_one, axis=1)
    grad_scale_one = jnp.sum(grad_hidden_one * normed_one, axis=1)
    tokens_grad = (
        grad_mid + norm_back(grad_hidden_one * (1.0 + scale_one), normed_one, inv_one)
    ).astype(jnp.bfloat16)
    slot_mod_grad = jnp.concatenate(
        [
            grad_shift_one,
            grad_scale_one,
            grad_gate_one,
            grad_shift_two,
            grad_scale_two,
            grad_gate_two,
        ],
        axis=-1,
    )
    mod_local = jnp.dot(slot_pick.T, slot_mod_grad, precision=highest)
    mod_grad = lax.psum(mod_local, ("dp", "grp"))
    mod_grad_cols = lax.dynamic_slice_in_dim(
        mod_grad, lax.axis_index("grp") * col_width, col_width, 1
    )
    ada_weight_grad = jnp.dot(silu_cond.T, mod_grad_cols, precision=highest)
    ada_offset_grad = jnp.sum(mod_grad_cols, axis=0)
    cond_partial = jnp.dot(mod_grad_cols, ada_weight.T, precision=highest)
    cond_total = lax.psum(cond_partial, "grp")
    sigmoid_cond = jax.nn.sigmoid(condition)
    condition_grad = cond_total * sigmoid_cond * (1.0 + condition * (1.0 - sigmoid_cond))
    data_count = lax.axis_size("dp")
    square_sums = lax.psum(
        (
            jnp.sum(ada_weight_grad * ada_weight_grad),
            jnp.sum(ada_offset_grad * ada_offset_grad) / data_count,
            jnp.sum(qkv_weight_grad * qkv_weight_grad),
            jnp.sum(proj_weight_grad * proj_weight_grad),
            jnp.sum(up_weight_grad * up_weight_grad),
            jnp.sum(down_weight_grad * down_weight_grad),
            jnp.sum(main_bias_grad * main_bias_grad),
        ),
        ("dp", "grp"),
    )
    entry_counts = (D * 6 * D, 6 * D, D * 3 * HW, HW * D, D * FF, FF * D, 2 * HW + 2 * D + FF)
    results = []
    for index_param, (weight, first_mom, second_mom, gradient) in enumerate(
        (
            (ada_weight, ada_weight_mean, ada_weight_square, ada_weight_grad),
            (ada_offset, ada_offset_mean, ada_offset_square, ada_offset_grad),
            (qkv_weight, qkv_weight_mean, qkv_weight_square, qkv_weight_grad),
            (proj_weight, proj_weight_mean, proj_weight_square, proj_weight_grad),
            (up_weight, up_weight_mean, up_weight_square, up_weight_grad),
            (down_weight, down_weight_mean, down_weight_square, down_weight_grad),
            (main_bias, main_bias_mean, main_bias_square, main_bias_grad),
        )
    ):
        factor = clip_from(square_sums[index_param], entry_counts[index_param])
        weight_new, first_new, second_new = adam_update(
            weight, first_mom, second_mom, gradient, factor
        )
        results.append((gradient, weight_new, first_new, second_new))
    return (
        block_out,
        tokens_grad,
        condition_grad,
        results[0][0],
        results[0][1],
        results[0][2],
        results[0][3],
        results[1][0],
        results[1][1],
        results[1][2],
        results[1][3],
        results[2][0],
        results[2][1],
        results[2][2],
        results[2][3],
        results[3][0],
        results[3][1],
        results[3][2],
        results[3][3],
        results[4][0],
        results[4][1],
        results[4][2],
        results[4][3],
        results[5][0],
        results[5][1],
        results[5][2],
        results[5][3],
        results[6][0],
        results[6][1],
        results[6][2],
        results[6][3],
    )


def solution(mesh):
    small = mesh.shape["dp"] == 16 and mesh.shape["grp"] == 2
    return jax.shard_map(
        local if small else local_general,
        mesh=mesh,
        in_specs=(
            P("dp", "grp", None),
            P("dp", "grp", None),
            P(None, "dp"),
            P("dp"),
            P("dp"),
            P("dp", "grp"),
            P("dp", "grp"),
            P("dp", "grp"),
            P("grp"),
            P("grp"),
            P("grp"),
            P("dp", "grp"),
            P("dp", "grp"),
            P("dp", "grp"),
            P("dp", "grp"),
            P("dp", "grp"),
            P("dp", "grp"),
            P("dp", "grp"),
            P("dp", "grp"),
            P("dp", "grp"),
            P("dp", "grp"),
            P("dp", "grp"),
            P("dp", "grp"),
            P(("dp", "grp")),
            P(("dp", "grp")),
            P(("dp", "grp")),
        ),
        out_specs=(
            P("dp", "grp", None),
            P("dp", "grp", None),
            P(None, "dp"),
            P("dp", "grp"),
            P("dp", "grp"),
            P("dp", "grp"),
            P("dp", "grp"),
            P("grp"),
            P("grp"),
            P("grp"),
            P("grp"),
            P("dp", "grp"),
            P("dp", "grp"),
            P("dp", "grp"),
            P("dp", "grp"),
            P("dp", "grp"),
            P("dp", "grp"),
            P("dp", "grp"),
            P("dp", "grp"),
            P("dp", "grp"),
            P("dp", "grp"),
            P("dp", "grp"),
            P("dp", "grp"),
            P("dp", "grp"),
            P("dp", "grp"),
            P("dp", "grp"),
            P("dp", "grp"),
            P(("dp", "grp")),
            P(("dp", "grp")),
            P(("dp", "grp")),
            P(("dp", "grp")),
        ),
        check_vma=False,
    )
```
